32 devices in a mesh: ctx: 8 (over y, x, core), head: 4 (over z).
Axes of the slice: x: 2, y: 2, z: 4, core: 2. Of those that a mesh axis runs over, the one named last changes fastest.
Arguments:
- ssm_input: bfloat16 [2048, 8192], P('ctx', 'head'), may hold values from -6 to 6
- gate_input: bfloat16 [2048, 8192], P('ctx', 'head'), may hold values from -6 to 6
- step_raw: float32 [2048, 128], P('ctx', 'head'), may hold values from -4 to 4
- b_matrix: bfloat16 [2048, 1024], P('ctx', 'head'), may hold values from -6 to 6
- c_matrix: bfloat16 [2048, 1024], P('ctx', 'head'), may hold values from -6 to 6
- step_bias: float32 [128], P('head'), may hold values from -6 to -4
- log_rate: float32 [128], P('head')
- skip_gain: float32 [128], P('head'), may hold values from 0.5 to 1.5
- norm_weight: float32 [8192], P('head'), may hold values from 0.5 to 1.5
- doc_resets: int32 [2048], P('ctx'), may hold values from 0 to 1, as said below
- grad_output: bfloat16 [2048, 8192], P('ctx', 'head'), may hold values from -6 to 6
Outputs:
- grad_input: bfloat16 [2048, 8192], P('ctx', 'head')
- grad_gate: bfloat16 [2048, 8192], P('ctx', 'head')
- grad_step: float32 [2048, 128], P('ctx', 'head')
- grad_b_matrix: float32 [2048, 1024], P('ctx', 'head')
- grad_c_matrix: float32 [2048, 1024], P('ctx', 'head')
The draws below stay inside these ranges and needn't reach their ends.
Inputs may be any that keep to these rules, and one draw needn't show every extreme that they name: `doc_resets`: exactly 4 positions hold 1, all of them among positions 1 to 127; all others hold 0.
All inputs are finite; a program needn't handle non-finite values.
Results may differ from the reference program's by a relative error of at most 0.001.
Values sent between devices are 32-bit elements; how exact they have to be, the bound alone decides.
A program may use at most 64 MiB of HBM per device.

```python
import jax
import jax.numpy as jnp
from jax import lax

HEADS = 128
HEAD_DIM = 64
STATE = 128
GROUPS = 8
SPAN = 256
DOCS = 4
TOK_DEV = 256
TOKENS = 2048
D_INNER = 8192


def draw_log_rate(key, part):
    key_pick, key_slow, key_fast = jax.random.split(key, 3)
    share = 0.5
    picked = jax.random.uniform(key_pick, (HEADS,), jnp.float32)
    slow_rate = jnp.log(20.0 / TOKENS) + jax.random.uniform(key_slow, (HEADS,), jnp.float32) * jnp.log(10.0)
    fast_rate = jax.random.uniform(key_fast, (HEADS,), jnp.float32) * jnp.log(8.0)
    return jnp.where(picked < share, slow_rate, fast_rate)


def draw_doc_resets(key, part):
    starts = jax.random.permutation(key, TOK_DEV // 2 - 1)[:DOCS] + 1
    return jnp.zeros((TOKENS,), jnp.int32).at[starts].set(1)


def steps_of(key, dims, cuts, low, largest):
    gain, own = 1.0, jax.random.fold_in(key, 6)
    for axis_at, blocks in cuts:
        steps = jnp.exp(jax.random.uniform(jax.random.fold_in(own, axis_at), (blocks,), jnp.float32, low / len(cuts), largest / len(cuts)))
        gain = gain * jnp.repeat(steps, dims[axis_at] // blocks).reshape([-1 if axis == axis_at else 1 for axis in range(len(dims))])
    return gain


def gaussian(rng, extent, deviation, limit, cuts=(), kind=jnp.bfloat16):
    array = deviation * jax.random.normal(rng, extent, jnp.float32)
    if cuts:
        array = array * steps_of(rng, extent, cuts, -0.22, 0.18)
    return jnp.clip(array, -limit, limit).astype(kind)


def setup_inputs(seed: int = 0) -> dict:
    arg_keys = jax.random.split(jax.random.key(seed), 12)
    ssm_input = gaussian(arg_keys[0], (TOKENS, D_INNER), 1.0, 6.0, ((0, 8), (1, 4)))
    gate_input = gaussian(arg_keys[1], (TOKENS, D_INNER), 1.0, 6.0, ((0, 8), (1, 4)))
    step_raw = gaussian(arg_keys[2], (TOKENS, HEADS), 1.0, 4.0, ((0, 8), (1, 4)), jnp.float32)
    b_matrix = gaussian(arg_keys[3], (TOKENS, GROUPS * STATE), 1.0, 6.0, ((0, 8), (1, 4)))
    c_matrix = gaussian(arg_keys[4], (TOKENS, GROUPS * STATE), 1.0, 6.0, ((0, 8), (1, 4)))
    step_bias = jnp.clip(-6.0 + 2.0 * jax.random.uniform(arg_keys[5], (HEADS,), jnp.float32) ** steps_of(arg_keys[5], (HEADS,), ((0, 4),), -0.2, 0.2), -6.0, -4.0)
    log_rate = draw_log_rate(jax.random.fold_in(arg_keys[11], 71), 0)
    skip_gain = jnp.clip(0.5 + 1.0 * jax.random.uniform(arg_keys[7], (HEADS,), jnp.float32) ** steps_of(arg_keys[7], (HEADS,), ((0, 4),), -0.2, 0.2), 0.5, 1.5)
    norm_weight = jnp.clip(0.5 + 1.0 * jax.random.uniform(arg_keys[8], (D_INNER,), jnp.float32) ** steps_of(arg_keys[8], (D_INNER,), ((0, 4),), -0.2, 0.2), 0.5, 1.5)
    doc_resets = draw_doc_resets(jax.random.fold_in(arg_keys[11], 71), 0)
    grad_output = gaussian(arg_keys[10], (TOKENS, D_INNER), 1.0, 6.0, ((0, 8), (1, 4)))
    return dict(ssm_input=ssm_input, gate_input=gate_input, step_raw=step_raw, b_matrix=b_matrix, c_matrix=c_matrix, step_bias=step_bias, log_rate=log_rate, skip_gain=skip_gain, norm_weight=norm_weight, doc_resets=doc_resets, grad_output=grad_output)


HIGHEST_PRECISION = lax.Precision.HIGHEST
EPSILON = 1e-05

def span_mix(x_span, dt_span, b_span, c_span, log_cum, segment):
    log_rows = jnp.moveaxis(log_cum, 0, -1)
    spread = log_rows[..., :, None] - log_rows[..., None, :]
    places = jnp.arange(x_span.shape[0], dtype=jnp.int32)
    keep_mask = ((places[:, None] >= places[None, :]) & (segment[:, None] == segment[None, :])).astype(jnp.float32)
    masked = jnp.exp(jnp.minimum(spread, 0.0)) * keep_mask
    scores = jnp.einsum('tgn,sgn->gts', c_span, b_span, precision=HIGHEST_PRECISION)
    weights = scores[:, None] * masked * jnp.moveaxis(dt_span, 0, -1)[..., None, :]
    return jnp.einsum('ghts,sghp->tghp', weights, x_span, precision=HIGHEST_PRECISION)

def layer_output(ssm_input, gate_input, step_raw, b_matrix, c_matrix, step_bias, log_rate, skip_gain, norm_weight, doc_resets):
    per_group = HEADS // GROUPS
    spans = TOKENS // SPAN
    step_size = jax.nn.softplus(step_raw + step_bias[None, :])
    decay_rate = (-jnp.exp(log_rate)).reshape(GROUPS, per_group)
    x_spans = ssm_input.reshape(spans, SPAN, GROUPS, per_group, HEAD_DIM)
    dt_spans = step_size.reshape(spans, SPAN, GROUPS, per_group)
    b_spans = b_matrix.reshape(spans, SPAN, GROUPS, STATE)
    c_spans = c_matrix.reshape(spans, SPAN, GROUPS, STATE)
    reset_spans = doc_resets.reshape(spans, SPAN)

    def advance(carry_state, pieces):
        x_span, dt_span, b_span, c_span, reset_span = pieces
        log_cum = jnp.cumsum(dt_span * decay_rate, axis=0)
        segment = jnp.cumsum(reset_span, dtype=jnp.int32)
        inner_part = span_mix(x_span, dt_span, b_span, c_span, log_cum, segment)
        opened = (segment == 0).astype(jnp.float32)
        entry_decay = jnp.exp(log_cum) * opened[:, None, None]
        carried = jnp.einsum('tgn,ghpn->tghp', c_span, carry_state, precision=HIGHEST_PRECISION) * entry_decay[..., None]
        closing = segment[-1]
        tail_decay = jnp.exp(log_cum[-1] - log_cum) * (segment == closing).astype(jnp.float32)[:, None, None]
        added_terms = jnp.einsum('sgh,sghp,sgn->ghpn', tail_decay * dt_span, x_span, b_span, precision=HIGHEST_PRECISION)
        through = jnp.exp(log_cum[-1]) * (closing == 0).astype(jnp.float32)
        return (through[..., None, None] * carry_state + added_terms, inner_part + carried)
    zero_state = jnp.zeros((GROUPS, per_group, HEAD_DIM, STATE), jnp.float32)
    _, mixed = lax.scan(jax.checkpoint(advance), zero_state, (x_spans, dt_spans, b_spans, c_spans, reset_spans))
    core_out = mixed.reshape(TOKENS, HEADS * HEAD_DIM) + ssm_input * jnp.repeat(skip_gain, HEAD_DIM)[None, :]
    gated = core_out * jax.nn.silu(gate_input)
    inv_rms = lax.rsqrt(lax.optimization_barrier(jnp.mean(gated * gated, axis=1, keepdims=True)) + EPSILON)
    return gated * inv_rms * norm_weight[None, :]

def reference(ssm_input, gate_input, step_raw, b_matrix, c_matrix, step_bias, log_rate, skip_gain, norm_weight, doc_resets, grad_output):

    def loss_map(x_value, gate_value, step_value, b_value, c_value):
        return layer_output(x_value, gate_value, step_value, b_value, c_value, step_bias, log_rate, skip_gain, norm_weight, doc_resets)
    _, backward = jax.vjp(loss_map, ssm_input.astype(jnp.float32), gate_input.astype(jnp.float32), step_raw, b_matrix.astype(jnp.float32), c_matrix.astype(jnp.float32))
    grad_x, grad_g, grad_s, grad_b, grad_c = backward(grad_output.astype(jnp.float32))
    return (grad_x.astype(jnp.bfloat16), grad_g.astype(jnp.bfloat16), grad_s, grad_b, grad_c)
```

```python
import functools

import jax
import jax.numpy as jnp
from jax import lax
from jax.experimental import pallas as pl
from jax.experimental.pallas import tpu as pltpu
from jax.sharding import PartitionSpec as P

HEAD_DIM = 64
STATE = 128
EPSILON = 1e-05
NCH = 4
F32 = jnp.float32
BF16 = jnp.bfloat16
MESH = pl.DeviceIdType.MESH


def dot(a, b):
    return lax.dot_general(a, b, (((1,), (0,)), ((), ())), preferred_element_type=F32)


def dot_t(a, b):
    return lax.dot_general(a, b, (((1,), (1,)), ((), ())), preferred_element_type=F32)


def split(v):
    hi = v.astype(BF16)
    return hi, (v - hi.astype(F32)).astype(BF16)


def split3(v):
    hi = v.astype(BF16)
    rest = v - hi.astype(F32)
    mid = rest.astype(BF16)
    return hi, mid, (rest - mid.astype(F32)).astype(BF16)


def iota(shape, axis):
    return lax.broadcasted_iota(jnp.int32, shape, axis)


def kernel(
    n_ctx, n_head, width,
    x_ref, gate_ref, step_ref, b_ref, c_ref, bias_ref, rate_ref, skip_ref, nw_ref, reset_ref, go_ref,
    gx_ref, gg_ref, gs_ref, gb_ref, gc_ref,
    loc, cbuf, tot, rbuf, obuf, entry,
    lcrep, rrep, lct, rt, negm, negmt, smat, smatt, dst,
    ybuf, dybuf, dyh_ref, dyl_ref, edh_ref, edl_ref, xsh_ref, xsl_ref, dxbuf, tdx, eexp,
    nsend, nrecv, send_sem, recv_sem, nsend_sem, nrecv_sem,
):
    T, HP = x_ref.shape
    H = step_ref.shape[1]
    G = b_ref.shape[1] // STATE
    per = H // G
    blocks = 2 * NCH
    CH = HP // blocks
    bpg = blocks // G
    bits = n_ctx.bit_length() - 1
    me = lax.axis_index("ctx")
    me_h = lax.axis_index("head")
    core = lax.rem(me, 2)
    other = 1 - core

    def partner(j):
        bit = lax.rem(me // (1 << j), 2)
        return me + (1 - 2 * bit) * (1 << j), bit

    barrier = pltpu.get_barrier_semaphore()
    for j in range(bits):
        pl.semaphore_signal(barrier, inc=1, device_id={"ctx": partner(j)[0]}, device_id_type=MESH)
    for d in range(1, n_head):
        pl.semaphore_signal(barrier, inc=1, device_id={"head": lax.rem(me_h + d, n_head)}, device_id_type=MESH)

    shifted = step_ref[...] + bias_ref[...]
    dt = jnp.maximum(shifted, 0.0) + jnp.log1p(jnp.exp(-jnp.abs(shifted)))
    sig_step = 1.0 / (1.0 + jnp.exp(-shifted))
    rate = -jnp.exp(rate_ref[...])
    tri = (iota((T, T), 0) >= iota((T, T), 1)).astype(F32).astype(BF16)
    triu = (iota((T, T), 0) <= iota((T, T), 1)).astype(F32).astype(BF16)
    lc = sum(dot(tri, part) for part in split3(dt * rate))
    rcol = jnp.log(dt) - lc
    lc_end = lc[T - 1 : T, :]
    r8 = jnp.broadcast_to(reset_ref[...].astype(F32), (8, T)).astype(BF16)
    seg_row = dot(r8, triu)[0:1, :]
    seg_col = dot_t(tri, r8)[:, 0:1]
    seg_end = seg_row[:, T - 1 : T]
    opened = (seg_col == 0.0).astype(F32)
    same_end = (seg_col == seg_end).astype(F32)
    through = jnp.exp(lc_end) * (seg_end == 0.0).astype(F32)
    e_col = jnp.exp(lc) * opened
    taudt = jnp.exp(lc_end - lc) * same_end * dt

    eh = (iota((H, HP), 1) // HEAD_DIM == iota((H, HP), 0)).astype(F32).astype(BF16)
    wide = (iota((H, H * 128), 1) // 128 == iota((H, H * 128), 0)).astype(F32).astype(BF16)
    eye = (iota((H, H), 0) == iota((H, H), 1)).astype(F32).astype(BF16)
    through8 = jnp.broadcast_to(through, (8, H))
    thx = sum(dot(part, eh) for part in split(through8))
    tdx[...] = sum(dot(part, eh) for part in split(taudt))
    for i in range(blocks):
        loc[0, i, STATE : STATE + 8, :] = thx[:, i * CH : (i + 1) * CH]
        loc[1, i, STATE : STATE + 8, :] = thx[:, i * CH : (i + 1) * CH]

    b_t = [b_ref[:, g * STATE : (g + 1) * STATE].astype(F32).T.astype(BF16) for g in range(G)]
    for i in range(blocks):
        lanes = slice(i * CH, (i + 1) * CH)
        hi, lo = split(tdx[:, lanes] * x_ref[:, lanes].astype(F32))
        xsh_ref[:, lanes] = hi
        xsl_ref[:, lanes] = lo
        bt = b_t[i // bpg]
        loc[0, i, 0:STATE, :] = dot(bt, hi) + dot(bt, lo)

    pl.semaphore_wait(barrier, bits + n_head - 1)

    def copy_to(way, slot, k, src, dst, device):
        return pltpu.make_async_remote_copy(
            src_ref=src, dst_ref=dst,
            send_sem=send_sem.at[way, slot, k], recv_sem=recv_sem.at[way, slot, k],
            device_id=device, device_id_type=MESH,
        )

    mate, _ = partner(0)

    def core_copy(way, k):
        return copy_to(way, 0, k, loc.at[way, other * NCH + k], cbuf.at[way, k], {"ctx": mate})

    def step_copy(way, j, k):
        return copy_to(way, j, k, tot.at[way, j - 1, k], rbuf.at[way, j - 1, k], {"ctx": partner(j)[0]})

    def out_copy(way, k):
        return copy_to(way, bits, k, obuf.at[way, k], entry.at[way, core * NCH + k], {"ctx": mate})

    S = STATE

    def exchange(way, work):
        own_first = (core == 0) if way == 0 else (core == 1)
        for k in range(NCH):
            core_copy(way, k).start()
        work(0)
        early_state, early_decay = [], []
        for k in range(NCH):
            core_copy(way, k).wait_recv()
            mine = loc[way, core * NCH + k]
            got = cbuf[way, k]
            early = jnp.where(own_first, mine, got)
            late = jnp.where(own_first, got, mine)
            dl = late[S : S + 1, :]
            tot[way, 0, k, 0:S, :] = dl * early[0:S, :] + late[0:S, :]
            tot[way, 0, k, S : S + 8, :] = late[S : S + 8, :] * early[S : S + 8, :]
            step_copy(way, 1, k).start()
        prefix = [None] * NCH
        for j in range(1, bits):
            bit = partner(j)[1]
            after = (bit == 1) if way == 0 else (bit == 0)
            for k in range(NCH):
                if j == 1:
                    work(k + 1)
                step_copy(way, j, k).wait_recv()
                got = rbuf[way, j - 1, k]
                if j == 1:
                    base = jnp.where(iota((S + 8, CH), 0) < S, 0.0, 1.0)
                else:
                    base = entry[way, core * NCH + k]
                moved = base[S : S + 1, :] * got
                new = jnp.where(iota((S + 8, CH), 0) < S, moved + base, moved)
                entry[way, core * NCH + k] = jnp.where(after, new, base)
                if j < bits - 1:
                    mine = tot[way, j - 1, k]
                    early = jnp.where(after, got, mine)
                    late = jnp.where(after, mine, got)
                    dl = late[S : S + 1, :]
                    tot[way, j, k, 0:S, :] = dl * early[0:S, :] + late[0:S, :]
                    tot[way, j, k, S : S + 8, :] = late[S : S + 8, :] * early[S : S + 8, :]
                    step_copy(way, j + 1, k).start()
                else:
                    mine = loc[way, core * NCH + k]
                    theirs = cbuf[way, k]
                    early = jnp.where(own_first, mine, theirs)
                    lead = entry[way, core * NCH + k]
                    trail = early[S : S + 1, :] * lead + early
                    obuf[way, k] = jnp.where(own_first, trail, lead)
                    entry[way, core * NCH + k] = jnp.where(own_first, lead, trail)
                    out_copy(way, k).start()
        for k in range(NCH):
            out_copy(way, k).wait_recv()
        for k in range(NCH):
            core_copy(way, k).wait_send()
            for j in range(1, bits):
                step_copy(way, j, k).wait_send()
            out_copy(way, k).wait_send()

    lane = iota((T, 128), 1)
    mask_a = (lane < HEAD_DIM).astype(F32).astype(BF16)
    mask_b = (lane >= HEAD_DIM).astype(F32).astype(BF16)
    pairs = H // 2

    def prepare():
        eexp[...] = sum(dot(part, eh) for part in split(e_col))
        lcrep[...] = sum(dot(part, wide) for part in split3(lc))
        rrep[...] = sum(dot(part, wide) for part in split3(rcol))
        lct[...] = sum(dot_t(eye, part) for part in split3(lc))
        rt[...] = sum(dot_t(eye, part) for part in split3(rcol))
        ok = (iota((T, T), 0) >= iota((T, T), 1)) & (seg_col == seg_row)
        negm[...] = jnp.where(ok, 0.0, -1e30)
        okt = (iota((T, T), 0) <= iota((T, T), 1)) & (seg_col == seg_row)
        negmt[...] = jnp.where(okt, 0.0, -1e30)
        for g in range(G):
            gs = slice(g * STATE, (g + 1) * STATE)
            smat[g] = dot_t(c_ref[:, gs], b_ref[:, gs])
            smatt[g] = dot_t(b_ref[:, gs], c_ref[:, gs])
            dst[g] = jnp.zeros((T, T), F32)

    def column(ref, h):
        col = ref[:, pl.ds(pl.multiple_of(h * 128, 128), 128)]
        return jnp.concatenate([col] * (T // 128), axis=1)

    def forward_pair(j, carry):
        lanes = pl.ds(pl.multiple_of(j * 128, 128), 128)
        xp = x_ref[:, lanes]
        s = smat[(2 * j) // per]
        neg = negm[...]
        y = None
        for half, mask in ((0, mask_a), (1, mask_b)):
            h = 2 * j + half
            w = jnp.exp(column(lcrep, h) + rt[pl.ds(h, 1), :] + neg) * s
            hi, lo = split(w)
            xm = xp * mask
            part = dot(hi, xm) + dot(lo, xm)
            y = part if y is None else y + part
        ybuf[:, lanes] = y
        return carry

    def backward_pair(j, carry):
        lanes = pl.ds(pl.multiple_of(j * 128, 128), 128)
        xp = x_ref[:, lanes]
        dyh = dyh_ref[:, lanes]
        dyl = dyl_ref[:, lanes]
        g = (2 * j) // per
        s = smatt[g]
        neg = negmt[...]
        dx = None
        acc = dst[g]
        for half, mask in ((0, mask_a), (1, mask_b)):
            h = 2 * j + half
            e = jnp.exp(column(rrep, h) + lct[pl.ds(h, 1), :] + neg)
            hi, lo = split(e * s)
            dh = dyh * mask
            part = dot(hi, dh) + dot(hi, dyl * mask) + dot(lo, dh)
            dx = part if dx is None else dx + part
            xm = xp * mask
            acc = acc + (dot_t(xm, dyh) + dot_t(xm, dyl)) * e
        dst[g] = acc
        dxbuf[:, lanes] = dx
        return carry

    def slices(run):
        bounds = [pairs * k // NCH for k in range(NCH + 1)]

        def work(k):
            if k > 0:
                lax.fori_loop(bounds[k - 1], bounds[k], run, 0)

        return work

    forward_work = slices(forward_pair)

    def first_work(k):
        if k == 0:
            prepare()
        forward_work(k)

    exchange(0, first_work)

    q_sum = jnp.zeros((T, CH), F32)
    p_sum = jnp.zeros((T, CH), F32)
    for i in range(blocks):
        lanes = slice(i * CH, (i + 1) * CH)
        g = i // bpg
        cg = c_ref[:, g * STATE : (g + 1) * STATE]
        hi, lo = split(entry[0, i, 0:STATE, :])
        y = ybuf[:, lanes] + (dot(cg, hi) + dot(cg, lo)) * eexp[:, lanes]
        ybuf[:, lanes] = y
        core_out = y + x_ref[:, lanes].astype(F32) * skip_ref[:, lanes]
        gate = gate_ref[:, lanes].astype(F32)
        gated = core_out * gate / (1.0 + jnp.exp(-gate))
        q_sum = q_sum + gated * gated
        p_sum = p_sum + gated * (nw_ref[:, lanes] * go_ref[:, lanes].astype(F32))
    ones8 = jnp.ones((8, CH), BF16)
    nsend[0:8, :] = sum(dot_t(ones8, part) for part in split3(q_sum))
    nsend[8:16, :] = sum(dot_t(ones8, part) for part in split3(p_sum))

    def norm_copy(d):
        return pltpu.make_async_remote_copy(
            src_ref=nsend, dst_ref=nrecv.at[d - 1],
            send_sem=nsend_sem.at[d - 1], recv_sem=nrecv_sem.at[d - 1],
            device_id={"head": lax.rem(me_h + d, n_head)}, device_id_type=MESH,
        )

    for d in range(1, n_head):
        norm_copy(d).start()
    c_t = [c_ref[:, g * STATE : (g + 1) * STATE].astype(F32).T.astype(BF16) for g in range(G)]
    sums = nsend[...]
    for d in range(1, n_head):
        norm_copy(d).wait_recv()
        sums = sums + nrecv[d - 1]
    inv_row = lax.rsqrt(sums[0:1, :] / width + EPSILON)
    coef_row = inv_row * inv_row * inv_row * sums[8:9, :] / width
    inv = jnp.broadcast_to(inv_row, (128, T)).T
    coef = jnp.broadcast_to(coef_row, (128, T)).T
    if CH > 128:
        inv = jnp.concatenate([inv] * (CH // 128), axis=1)
        coef = jnp.concatenate([coef] * (CH // 128), axis=1)

    dyy = jnp.zeros((T, H), F32)
    for i in range(blocks):
        lanes = slice(i * CH, (i + 1) * CH)
        g = i // bpg
        y = ybuf[:, lanes]
        core_out = y + x_ref[:, lanes].astype(F32) * skip_ref[:, lanes]
        gate = gate_ref[:, lanes].astype(F32)
        sig = 1.0 / (1.0 + jnp.exp(-gate))
        act = gate * sig
        weighted = nw_ref[:, lanes] * go_ref[:, lanes].astype(F32)
        ggated = inv * weighted - core_out * act * coef
        dy = ggated * act
        gg_ref[:, lanes] = (ggated * core_out * sig * (1.0 + gate * (1.0 - sig))).astype(BF16)
        dybuf[:, lanes] = dy
        dyh_ref[:, lanes], dyl_ref[:, lanes] = split(dy)
        hi, lo = split(dy * eexp[:, lanes])
        edh_ref[:, lanes] = hi
        edl_ref[:, lanes] = lo
        loc[1, i, 0:STATE, :] = dot(c_t[g], hi) + dot(c_t[g], lo)
        dyy = dyy + sum(dot_t(part, eh[:, lanes]) for part in split(dy * y))

    backward_work = slices(backward_pair)
    exchange(1, backward_work)

    for g in range(G):
        gs = slice(g * STATE, (g + 1) * STATE)
        acc = dst[g]
        hi, lo = split(acc)
        cg = c_ref[:, gs]
        gb = dot(hi, cg) + dot(lo, cg)
        hi, lo = split(acc.T)
        bg = b_ref[:, gs]
        gc = dot(hi, bg) + dot(lo, bg)
        for i in range(g * bpg, (g + 1) * bpg):
            lanes = slice(i * CH, (i + 1) * CH)
            hi, lo = split(entry[0, i, 0:STATE, :])
            edh = edh_ref[:, lanes]
            gc = gc + dot_t(edh, hi) + dot_t(edh, lo) + dot_t(edl_ref[:, lanes], hi)
            hi, lo = split(entry[1, i, 0:STATE, :])
            xsh = xsh_ref[:, lanes]
            gb = gb + dot_t(xsh, hi) + dot_t(xsh, lo) + dot_t(xsl_ref[:, lanes], hi)
        gb_ref[:, gs] = gb
        gc_ref[:, gs] = gc

    xdx = jnp.zeros((T, H), F32)
    ends = jnp.zeros((8, H), F32)
    for i in range(blocks):
        lanes = slice(i * CH, (i + 1) * CH)
        g = i // bpg
        bg = b_ref[:, g * STATE : (g + 1) * STATE]
        adj = entry[1, i, 0:STATE, :]
        hi, lo = split(adj)
        dx = dxbuf[:, lanes] + (dot(bg, hi) + dot(bg, lo)) * tdx[:, lanes]
        gx_ref[:, lanes] = (dx + dybuf[:, lanes] * skip_ref[:, lanes]).astype(BF16)
        xdx = xdx + sum(dot_t(part, eh[:, lanes]) for part in split(dx * x_ref[:, lanes].astype(F32)))
        local = loc[0, i]
        leaving = local[S : S + 1, :] * entry[0, i, 0:STATE, :] + local[0:S, :]
        col = jnp.sum(adj * leaving, axis=0, keepdims=True)
        col = jnp.broadcast_to(col, (8, CH))
        ends = ends + sum(dot_t(part, eh[:, lanes]) for part in split3(col))
    rc = sum(dot(triu, part) for part in split3(dyy - xdx)) + ends[0:1, :]
    gs_ref[...] = (xdx / dt + rate * rc) * sig_step

    for d in range(1, n_head):
        norm_copy(d).wait_send()


def body(mesh_shape, x, gate, step, b, c, bias, rate, skip, nw, resets, go):
    n_ctx, n_head = mesh_shape
    T, HP = x.shape
    H = step.shape[1]
    G = b.shape[1] // STATE
    bits = n_ctx.bit_length() - 1
    CH = HP // (2 * NCH)
    R = STATE + 8
    vm = pltpu.VMEM
    skip_cols = jnp.repeat(skip, HEAD_DIM)[None, :]
    return pl.pallas_call(
        functools.partial(kernel, n_ctx, n_head, HP * n_head),
        out_shape=(
            jax.ShapeDtypeStruct((T, HP), BF16),
            jax.ShapeDtypeStruct((T, HP), BF16),
            jax.ShapeDtypeStruct((T, H), F32),
            jax.ShapeDtypeStruct((T, G * STATE), F32),
            jax.ShapeDtypeStruct((T, G * STATE), F32),
        ),
        in_specs=[pl.BlockSpec(memory_space=pltpu.VMEM)] * 11,
        out_specs=[pl.BlockSpec(memory_space=pltpu.VMEM)] * 5,
        scratch_shapes=[
            vm((2, 2 * NCH, R, CH), F32),
            vm((2, NCH, R, CH), F32),
            vm((2, bits - 1, NCH, R, CH), F32),
            vm((2, bits - 1, NCH, R, CH), F32),
            vm((2, NCH, R, CH), F32),
            vm((2, 2 * NCH, R, CH), F32),
            vm((T, H * 128), F32),
            vm((T, H * 128), F32),
            vm((H, T), F32),
            vm((H, T), F32),
            vm((T, T), F32),
            vm((T, T), F32),
            vm((G, T, T), F32),
            vm((G, T, T), F32),
            vm((G, T, T), F32),
            vm((T, HP), F32),
            vm((T, HP), F32),
            vm((T, HP), BF16),
            vm((T, HP), BF16),
            vm((T, HP), BF16),
            vm((T, HP), BF16),
            vm((T, HP), BF16),
            vm((T, HP), BF16),
            vm((T, HP), F32),
            vm((T, HP), F32),
            vm((T, HP), F32),
            vm((16, T), F32),
            vm((max(n_head - 1, 1), 16, T), F32),
            pltpu.SemaphoreType.DMA((2, bits + 1, NCH)),
            pltpu.SemaphoreType.DMA((2, bits + 1, NCH)),
            pltpu.SemaphoreType.DMA((max(n_head - 1, 1),)),
            pltpu.SemaphoreType.DMA((max(n_head - 1, 1),)),
        ],
        compiler_params=pltpu.CompilerParams(
            collective_id=0, has_side_effects=True, vmem_limit_bytes=60 * 1024 * 1024
        ),
    )(
        x, gate, step, b, c, bias[None, :], rate[None, :], skip_cols, nw[None, :], resets[None, :], go
    )


def solution(mesh):
    return jax.shard_map(
        functools.partial(body, (mesh.shape["ctx"], mesh.shape["head"])),
        mesh=mesh,
        in_specs=(
            P("ctx", "head"), P("ctx", "head"), P("ctx", "head"), P("ctx", "head"), P("ctx", "head"),
            P("head"), P("head"), P("head"), P("head"), P("ctx"), P("ctx", "head"),
        ),
        out_specs=(P("ctx", "head"),) * 5,
        check_vma=False,
    )
```

```python
import functools

import jax
import jax.numpy as jnp
from jax import lax
from jax.experimental import pallas as pl
from jax.experimental.pallas import tpu as pltpu
from jax.sharding import PartitionSpec as P

HEAD_DIM = 64
STATE = 128
EPSILON = 1e-05
NCH = 4
F32 = jnp.float32
BF16 = jnp.bfloat16
MESH = pl.DeviceIdType.MESH


def dot(a, b):
    return lax.dot_general(a, b, (((1,), (0,)), ((), ())), preferred_element_type=F32)


def dot_t(a, b):
    return lax.dot_general(a, b, (((1,), (1,)), ((), ())), preferred_element_type=F32)


def split(v):
    hi = v.astype(BF16)
    return hi, (v - hi.astype(F32)).astype(BF16)


def split3(v):
    hi = v.astype(BF16)
    rest = v - hi.astype(F32)
    mid = rest.astype(BF16)
    return hi, mid, (rest - mid.astype(F32)).astype(BF16)


def iota(shape, axis):
    return lax.broadcasted_iota(jnp.int32, shape, axis)


def kernel(
    n_ctx, n_head, width,
    x_ref, gate_ref, step_ref, b_ref, c_ref, bias_ref, rate_ref, skip_ref, nw_ref, reset_ref, go_ref,
    gx_ref, gg_ref, gs_ref, gb_ref, gc_ref,
    loc, cbuf, tot, rbuf, obuf, entry,
    lcrep, rrep, lct, rt, negm, negmt, smat, smatt, dst,
    ybuf, dybuf, dyh_ref, dyl_ref, edh_ref, edl_ref, xsh_ref, xsl_ref, dxbuf, tdx, eexp,
    btr, ctr, actb, wb, qacc, pacc, dyya, xdxa, nsend, nrecv, send_sem, recv_sem, nsend_sem, nrecv_sem,
):
    T, HP = x_ref.shape
    H = step_ref.shape[1]
    G = b_ref.shape[1] // STATE
    per = H // G
    blocks = 2 * NCH
    CH = HP // blocks
    bpg = blocks // G
    bits = n_ctx.bit_length() - 1
    me = lax.axis_index("ctx")
    me_h = lax.axis_index("head")
    core = lax.rem(me, 2)
    other = 1 - core

    def partner(j):
        bit = lax.rem(me // (1 << j), 2)
        return me + (1 - 2 * bit) * (1 << j), bit

    barrier = pltpu.get_barrier_semaphore()
    for j in range(bits):
        pl.semaphore_signal(barrier, inc=1, device_id={"ctx": partner(j)[0]}, device_id_type=MESH)
    for d in range(1, n_head):
        pl.semaphore_signal(barrier, inc=1, device_id={"head": lax.rem(me_h + d, n_head)}, device_id_type=MESH)

    shifted = step_ref[...] + bias_ref[...]
    dt = jnp.maximum(shifted, 0.0) + jnp.log1p(jnp.exp(-jnp.abs(shifted)))
    sig_step = 1.0 / (1.0 + jnp.exp(-shifted))
    rate = -jnp.exp(rate_ref[...])
    tri = (iota((T, T), 0) >= iota((T, T), 1)).astype(F32).astype(BF16)
    triu = (iota((T, T), 0) <= iota((T, T), 1)).astype(F32).astype(BF16)
    lc = sum(dot(tri, part) for part in split3(dt * rate))
    rcol = jnp.log(dt) - lc
    lc_end = lc[T - 1 : T, :]
    r8 = jnp.broadcast_to(reset_ref[...].astype(F32), (8, T)).astype(BF16)
    seg_row = dot(r8, triu)[0:1, :]
    seg_col = dot_t(tri, r8)[:, 0:1]
    seg_end = seg_row[:, T - 1 : T]
    opened = (seg_col == 0.0).astype(F32)
    same_end = (seg_col == seg_end).astype(F32)
    through = jnp.exp(lc_end) * (seg_end == 0.0).astype(F32)
    e_col = jnp.exp(lc) * opened
    taudt = jnp.exp(lc_end - lc) * same_end * dt

    eh = (iota((H, HP), 1) // HEAD_DIM == iota((H, HP), 0)).astype(F32).astype(BF16)
    wide = (iota((H, H * 128), 1) // 128 == iota((H, H * 128), 0)).astype(F32).astype(BF16)
    eye = (iota((H, H), 0) == iota((H, H), 1)).astype(F32).astype(BF16)
    through8 = jnp.broadcast_to(through, (8, H))
    thx = sum(dot(part, eh) for part in split(through8))
    tdx[...] = sum(dot(part, eh) for part in split(taudt))
    for i in range(blocks):
        loc[0, i, STATE : STATE + 8, :] = thx[:, i * CH : (i + 1) * CH]
        loc[1, i, STATE : STATE + 8, :] = thx[:, i * CH : (i + 1) * CH]

    for g in range(G):
        gs = slice(g * STATE, (g + 1) * STATE)
        btr[g] = b_ref[:, gs].astype(F32).T.astype(BF16)
        ctr[g] = c_ref[:, gs].astype(F32).T.astype(BF16)

    def lanes_of(i):
        return pl.ds(pl.multiple_of(i * CH, CH), CH)

    def group_of(i):
        return pl.ds(pl.multiple_of((i // bpg) * STATE, STATE), STATE)

    def heads_of(i):
        first = i * (CH // HEAD_DIM)
        return (iota((H, CH), 1) // HEAD_DIM + first == iota((H, CH), 0)).astype(F32).astype(BF16)

    def local_state(i):
        lanes = lanes_of(i)
        hi, lo = split(tdx[:, lanes] * x_ref[:, lanes].astype(F32))
        xsh_ref[:, lanes] = hi
        xsl_ref[:, lanes] = lo
        bt = btr[i // bpg]
        loc[0, i, 0:STATE, :] = dot(bt, hi) + dot(bt, lo)

    pl.semaphore_wait(barrier, bits + n_head - 1)

    def copy_to(way, slot, k, src, dst, device):
        return pltpu.make_async_remote_copy(
            src_ref=src, dst_ref=dst,
            send_sem=send_sem.at[way, slot, k], recv_sem=recv_sem.at[way, slot, k],
            device_id=device, device_id_type=MESH,
        )

    mate, _ = partner(0)

    def core_copy(way, k):
        return copy_to(way, 0, k, loc.at[way, other * NCH + k], cbuf.at[way, k], {"ctx": mate})

    def step_copy(way, j, k):
        return copy_to(way, j, k, tot.at[way, j - 1, k], rbuf.at[way, j - 1, k], {"ctx": partner(j)[0]})

    def out_copy(way, k):
        return copy_to(way, bits, k, obuf.at[way, k], entry.at[way, core * NCH + k], {"ctx": mate})

    S = STATE

    def exchange(way, produce, work, done):
        own_first = (core == 0) if way == 0 else (core == 1)
        for k in range(NCH):
            produce(other * NCH + k)
            core_copy(way, k).start()
        for k in range(NCH):
            produce(core * NCH + k)
        for k in range(NCH):
            core_copy(way, k).wait_recv()
            mine = loc[way, core * NCH + k]
            got = cbuf[way, k]
            early = jnp.where(own_first, mine, got)
            late = jnp.where(own_first, got, mine)
            dl = late[S : S + 1, :]
            tot[way, 0, k, 0:S, :] = dl * early[0:S, :] + late[0:S, :]
            tot[way, 0, k, S : S + 8, :] = late[S : S + 8, :] * early[S : S + 8, :]
            step_copy(way, 1, k).start()
        work(0)
        for j in range(1, bits):
            bit = partner(j)[1]
            after = (bit == 1) if way == 0 else (bit == 0)
            for k in range(NCH):
                step_copy(way, j, k).wait_recv()
                got = rbuf[way, j - 1, k]
                if j == 1:
                    base = jnp.where(iota((S + 8, CH), 0) < S, 0.0, 1.0)
                else:
                    base = entry[way, core * NCH + k]
                moved = base[S : S + 1, :] * got
                new = jnp.where(iota((S + 8, CH), 0) < S, moved + base, moved)
                entry[way, core * NCH + k] = jnp.where(after, new, base)
                if j < bits - 1:
                    mine = tot[way, j - 1, k]
                    early = jnp.where(after, got, mine)
                    late = jnp.where(after, mine, got)
                    dl = late[S : S + 1, :]
                    tot[way, j, k, 0:S, :] = dl * early[0:S, :] + late[0:S, :]
                    tot[way, j, k, S : S + 8, :] = late[S : S + 8, :] * early[S : S + 8, :]
                    step_copy(way, j + 1, k).start()
                    if j == 1:
                        work(k + 1)
                else:
                    mine = loc[way, core * NCH + k]
                    theirs = cbuf[way, k]
                    early = jnp.where(own_first, mine, theirs)
                    lead = entry[way, core * NCH + k]
                    trail = early[S : S + 1, :] * lead + early
                    obuf[way, k] = jnp.where(own_first, trail, lead)
                    entry[way, core * NCH + k] = jnp.where(own_first, lead, trail)
                    out_copy(way, k).start()
                    done(core * NCH + k)
            if j == 1:
                work(NCH + 1)
        for k in range(NCH):
            out_copy(way, k).wait_recv()
            done(other * NCH + k)
        for k in range(NCH):
            core_copy(way, k).wait_send()
            for j in range(1, bits):
                step_copy(way, j, k).wait_send()
            out_copy(way, k).wait_send()

    lane = iota((T, 128), 1)
    mask_a = (lane < HEAD_DIM).astype(F32).astype(BF16)
    mask_b = (lane >= HEAD_DIM).astype(F32).astype(BF16)
    pairs = H // 2

    def prepare():
        eexp[...] = sum(dot(part, eh) for part in split(e_col))
        lcrep[...] = sum(dot(part, wide) for part in split3(lc))
        rrep[...] = sum(dot(part, wide) for part in split3(rcol))
        lct[...] = sum(dot_t(eye, part) for part in split3(lc))
        rt[...] = sum(dot_t(eye, part) for part in split3(rcol))
        ok = (iota((T, T), 0) >= iota((T, T), 1)) & (seg_col == seg_row)
        negm[...] = jnp.where(ok, 0.0, -1e30)
        okt = (iota((T, T), 0) <= iota((T, T), 1)) & (seg_col == seg_row)
        negmt[...] = jnp.where(okt, 0.0, -1e30)
        for g in range(G):
            gs = slice(g * STATE, (g + 1) * STATE)
            smat[g] = dot_t(c_ref[:, gs], b_ref[:, gs])
            smatt[g] = dot_t(b_ref[:, gs], c_ref[:, gs])
            dst[g] = jnp.zeros((T, T), F32)

    def column(ref, h):
        col = ref[:, pl.ds(pl.multiple_of(h * 128, 128), 128)]
        return jnp.concatenate([col] * (T // 128), axis=1)

    def forward_pair(j, carry):
        lanes = pl.ds(pl.multiple_of(j * 128, 128), 128)
        xp = x_ref[:, lanes]
        s = smat[(2 * j) // per]
        neg = negm[...]
        y = None
        for half, mask in ((0, mask_a), (1, mask_b)):
            h = 2 * j + half
            w = jnp.exp(column(lcrep, h) + rt[pl.ds(h, 1), :] + neg) * s
            hi, lo = split(w)
            xm = xp * mask
            part = dot(hi, xm) + dot(lo, xm)
            y = part if y is None else y + part
        ybuf[:, lanes] = y
        return carry

    def backward_pair(j, carry):
        lanes = pl.ds(pl.multiple_of(j * 128, 128), 128)
        xp = x_ref[:, lanes]
        dyh = dyh_ref[:, lanes]
        dyl = dyl_ref[:, lanes]
        g = (2 * j) // per
        s = smatt[g]
        neg = negmt[...]
        dx = None
        acc = dst[g]
        for half, mask in ((0, mask_a), (1, mask_b)):
            h = 2 * j + half
            e = jnp.exp(column(rrep, h) + lct[pl.ds(h, 1), :] + neg)
            hi, lo = split(e * s)
            dh = dyh * mask
            part = dot(hi, dh) + dot(hi, dyl * mask) + dot(lo, dh)
            dx = part if dx is None else dx + part
            xm = xp * mask
            acc = acc + (dot_t(xm, dyh) + dot_t(xm, dyl)) * e
        dst[g] = acc
        dxbuf[:, lanes] = dx
        return carry

    def slices(run):
        bounds = [pairs * k // NCH for k in range(NCH + 1)]

        def work(k):
            if 0 < k <= NCH:
                lax.fori_loop(bounds[k - 1], bounds[k], run, 0)

        return work

    forward_work = slices(forward_pair)

    def first_work(k):
        if k == 0:
            prepare()
        forward_work(k)
        if 0 < k <= NCH:
            for i in (2 * k - 2, 2 * k - 1):
                lanes = lanes_of(i)
                gate = gate_ref[:, lanes].astype(F32)
                actb[:, lanes] = gate / (1.0 + jnp.exp(-gate))
                wb[:, lanes] = nw_ref[:, lanes] * go_ref[:, lanes].astype(F32)

    qacc[...] = jnp.zeros((T, CH), F32)
    pacc[...] = jnp.zeros((T, CH), F32)

    def gate_block(i):
        lanes = lanes_of(i)
        cg = c_ref[:, group_of(i)]
        hi, lo = split(entry[0, i, 0:STATE, :])
        y = ybuf[:, lanes] + (dot(cg, hi) + dot(cg, lo)) * eexp[:, lanes]
        ybuf[:, lanes] = y
        gated = (y + x_ref[:, lanes].astype(F32) * skip_ref[:, lanes]) * actb[:, lanes]
        qacc[...] += gated * gated
        pacc[...] += gated * wb[:, lanes]

    exchange(0, local_state, first_work, gate_block)

    q_sum = qacc[...]
    p_sum = pacc[...]
    ones8 = jnp.ones((8, CH), BF16)
    nsend[0:8, :] = sum(dot_t(ones8, part) for part in split3(q_sum))
    nsend[8:16, :] = sum(dot_t(ones8, part) for part in split3(p_sum))

    def norm_copy(d):
        return pltpu.make_async_remote_copy(
            src_ref=nsend, dst_ref=nrecv.at[d - 1],
            send_sem=nsend_sem.at[d - 1], recv_sem=nrecv_sem.at[d - 1],
            device_id={"head": lax.rem(me_h + d, n_head)}, device_id_type=MESH,
        )

    for d in range(1, n_head):
        norm_copy(d).start()
    sums = nsend[...]
    for d in range(1, n_head):
        norm_copy(d).wait_recv()
        sums = sums + nrecv[d - 1]
    inv_row = lax.rsqrt(sums[0:1, :] / width + EPSILON)
    coef_row = inv_row * inv_row * inv_row * sums[8:9, :] / width
    inv = jnp.broadcast_to(inv_row, (128, T)).T
    coef = jnp.broadcast_to(coef_row, (128, T)).T
    if CH > 128:
        inv = jnp.concatenate([inv] * (CH // 128), axis=1)
        coef = jnp.concatenate([coef] * (CH // 128), axis=1)

    def adjoint_block(i):
        lanes = lanes_of(i)
        act = actb[:, lanes]
        gated = (ybuf[:, lanes] + x_ref[:, lanes].astype(F32) * skip_ref[:, lanes]) * act
        dy = (inv * wb[:, lanes] - gated * coef) * act
        dybuf[:, lanes] = dy
        dyh_ref[:, lanes], dyl_ref[:, lanes] = split(dy)
        hi, lo = split(dy * eexp[:, lanes])
        edh_ref[:, lanes] = hi
        edl_ref[:, lanes] = lo
        ct = ctr[i // bpg]
        loc[1, i, 0:STATE, :] = dot(ct, hi) + dot(ct, lo)

    dyya[...] = jnp.zeros((T, H), F32)
    xdxa[...] = jnp.zeros((T, H), F32)

    def gate_grad(i):
        lanes = lanes_of(i)
        y = ybuf[:, lanes]
        core_out = y + x_ref[:, lanes].astype(F32) * skip_ref[:, lanes]
        gate = gate_ref[:, lanes].astype(F32)
        sig = 1.0 / (1.0 + jnp.exp(-gate))
        ggated = inv * wb[:, lanes] - core_out * actb[:, lanes] * coef
        gg_ref[:, lanes] = (ggated * core_out * sig * (1.0 + gate * (1.0 - sig))).astype(BF16)
        dyya[...] += sum(dot_t(part, heads_of(i)) for part in split(dybuf[:, lanes] * y))

    backward_work = slices(backward_pair)

    def second_work(k):
        backward_work(k)
        if k == 0:
            for i in range(NCH):
                gate_grad(i)
        elif k <= NCH:
            gate_grad(NCH + k - 1)
        else:
            for g in range(G):
                gs = slice(g * STATE, (g + 1) * STATE)
                acc = dst[g]
                hi, lo = split(acc)
                cg = c_ref[:, gs]
                gb_ref[:, gs] = dot(hi, cg) + dot(lo, cg)
                hi, lo = split(acc.T)
                bg = b_ref[:, gs]
                gc = dot(hi, bg) + dot(lo, bg)
                for i in range(g * bpg, (g + 1) * bpg):
                    lanes = lanes_of(i)
                    hi, lo = split(entry[0, i, 0:STATE, :])
                    edh = edh_ref[:, lanes]
                    gc = gc + dot_t(edh, hi) + dot_t(edh, lo) + dot_t(edl_ref[:, lanes], hi)
                gc_ref[:, gs] = gc

    ends_of = []

    def input_block(i):
        lanes = lanes_of(i)
        gs = group_of(i)
        bg = b_ref[:, gs]
        adj = entry[1, i, 0:STATE, :]
        hi, lo = split(adj)
        xsh = xsh_ref[:, lanes]
        gb_ref[:, gs] += dot_t(xsh, hi) + dot_t(xsh, lo) + dot_t(xsl_ref[:, lanes], hi)
        dx = dxbuf[:, lanes] + (dot(bg, hi) + dot(bg, lo)) * tdx[:, lanes]
        gx_ref[:, lanes] = (dx + dybuf[:, lanes] * skip_ref[:, lanes]).astype(BF16)
        eb = heads_of(i)
        xdxa[...] += sum(dot_t(part, eb) for part in split(dx * x_ref[:, lanes].astype(F32)))
        local = loc[0, i]
        leaving = local[S : S + 1, :] * entry[0, i, 0:STATE, :] + local[0:S, :]
        col = jnp.broadcast_to(jnp.sum(adj * leaving, axis=0, keepdims=True), (8, CH))
        ends_of.append(sum(dot_t(part, eb) for part in split3(col)))

    exchange(1, adjoint_block, second_work, input_block)
    ends = sum(ends_of)
    xdx = xdxa[...]
    dyy = dyya[...]
    rc = sum(dot(triu, part) for part in split3(dyy - xdx)) + ends[0:1, :]
    gs_ref[...] = (xdx / dt + rate * rc) * sig_step

    for d in range(1, n_head):
        norm_copy(d).wait_send()


def body(mesh_shape, x, gate, step, b, c, bias, rate, skip, nw, resets, go):
    n_ctx, n_head = mesh_shape
    T, HP = x.shape
    H = step.shape[1]
    G = b.shape[1] // STATE
    bits = n_ctx.bit_length() - 1
    CH = HP // (2 * NCH)
    R = STATE + 8
    vm = pltpu.VMEM
    skip_cols = jnp.repeat(skip, HEAD_DIM)[None, :]
    return pl.pallas_call(
        functools.partial(kernel, n_ctx, n_head, HP * n_head),
        out_shape=(
            jax.ShapeDtypeStruct((T, HP), BF16),
            jax.ShapeDtypeStruct((T, HP), BF16),
            jax.ShapeDtypeStruct((T, H), F32),
            jax.ShapeDtypeStruct((T, G * STATE), F32),
            jax.ShapeDtypeStruct((T, G * STATE), F32),
        ),
        in_specs=[pl.BlockSpec(memory_space=pltpu.VMEM)] * 11,
        out_specs=[pl.BlockSpec(memory_space=pltpu.VMEM)] * 5,
        scratch_shapes=[
            vm((2, 2 * NCH, R, CH), F32),
            vm((2, NCH, R, CH), F32),
            vm((2, bits - 1, NCH, R, CH), F32),
            vm((2, bits - 1, NCH, R, CH), F32),
            vm((2, NCH, R, CH), F32),
            vm((2, 2 * NCH, R, CH), F32),
            vm((T, H * 128), F32),
            vm((T, H * 128), F32),
            vm((H, T), F32),
            vm((H, T), F32),
            vm((T, T), F32),
            vm((T, T), F32),
            vm((G, T, T), F32),
            vm((G, T, T), F32),
            vm((G, T, T), F32),
            vm((T, HP), F32),
            vm((T, HP), F32),
            vm((T, HP), BF16),
            vm((T, HP), BF16),
            vm((T, HP), BF16),
            vm((T, HP), BF16),
            vm((T, HP), BF16),
            vm((T, HP), BF16),
            vm((T, HP), F32),
            vm((T, HP), F32),
            vm((T, HP), F32),
            vm((G, STATE, T), BF16),
            vm((G, STATE, T), BF16),
            vm((T, HP), F32),
            vm((T, HP), F32),
            vm((T, CH), F32),
            vm((T, CH), F32),
            vm((T, H), F32),
            vm((T, H), F32),
            vm((16, T), F32),
            vm((max(n_head - 1, 1), 16, T), F32),
            pltpu.SemaphoreType.DMA((2, bits + 1, NCH)),
            pltpu.SemaphoreType.DMA((2, bits + 1, NCH)),
            pltpu.SemaphoreType.DMA((max(n_head - 1, 1),)),
            pltpu.SemaphoreType.DMA((max(n_head - 1, 1),)),
        ],
        compiler_params=pltpu.CompilerParams(
            collective_id=0, has_side_effects=True, vmem_limit_bytes=60 * 1024 * 1024
        ),
    )(
        x, gate, step, b, c, bias[None, :], rate[None, :], skip_cols, nw[None, :], resets[None, :], go
    )


def solution(mesh):
    return jax.shard_map(
        functools.partial(body, (mesh.shape["ctx"], mesh.shape["head"])),
        mesh=mesh,
        in_specs=(
            P("ctx", "head"), P("ctx", "head"), P("ctx", "head"), P("ctx", "head"), P("ctx", "head"),
            P("head"), P("head"), P("head"), P("head"), P("ctx"), P("ctx", "head"),
        ),
        out_specs=(P("ctx", "head"),) * 5,
        check_vma=False,
    )
```

```python
import functools

import jax
import jax.numpy as jnp
from jax import lax
from jax.experimental import pallas as pl
from jax.experimental.pallas import tpu as pltpu
from jax.sharding import PartitionSpec as P

HEAD_DIM = 64
STATE = 128
EPSILON = 1e-05
NCH = 4
F32 = jnp.float32
BF16 = jnp.bfloat16
MESH = pl.DeviceIdType.MESH


def dot(a, b):
    return lax.dot_general(a, b, (((1,), (0,)), ((), ())), preferred_element_type=F32)


def dot_t(a, b):
    return lax.dot_general(a, b, (((1,), (1,)), ((), ())), preferred_element_type=F32)


def split(v):
    hi = v.astype(BF16)
    return hi, (v - hi.astype(F32)).astype(BF16)


def split3(v):
    hi = v.astype(BF16)
    rest = v - hi.astype(F32)
    mid = rest.astype(BF16)
    return hi, mid, (rest - mid.astype(F32)).astype(BF16)


def iota(shape, axis):
    return lax.broadcasted_iota(jnp.int32, shape, axis)


def kernel(
    n_ctx, n_head, width,
    x_ref, gate_ref, step_ref, b_ref, c_ref, bias_ref, rate_ref, skip_ref, nw_ref, reset_ref, go_ref,
    gx_ref, gg_ref, gs_ref, gb_ref, gc_ref,
    loc, cbuf, tot, rbuf, obuf, entry,
    lcrep, rrep, lct, rt, negm, negmt, smat, smatt, dst,
    ybuf, dybuf, dyh_ref, dyl_ref, edh_ref, edl_ref, xsh_ref, xsl_ref, dxbuf, tdx, eexp,
    btr, ctr, actb, wb, qacc, pacc, dyya, xdxa, nsend, nrecv, send_sem, recv_sem, nsend_sem, nrecv_sem,
):
    T, HP = x_ref.shape
    H = step_ref.shape[1]
    G = b_ref.shape[1] // STATE
    per = H // G
    blocks = 2 * NCH
    CH = HP // blocks
    bpg = blocks // G
    bits = n_ctx.bit_length() - 1
    me = lax.axis_index("ctx")
    me_h = lax.axis_index("head")
    core = lax.rem(me, 2)
    other = 1 - core

    def partner(j):
        bit = lax.rem(me // (1 << j), 2)
        return me + (1 - 2 * bit) * (1 << j), bit

    barrier = pltpu.get_barrier_semaphore()
    for j in range(bits):
        pl.semaphore_signal(barrier, inc=1, device_id={"ctx": partner(j)[0]}, device_id_type=MESH)
    for d in range(1, n_head):
        pl.semaphore_signal(barrier, inc=1, device_id={"head": lax.rem(me_h + d, n_head)}, device_id_type=MESH)

    shifted = step_ref[...] + bias_ref[...]
    dt = jnp.maximum(shifted, 0.0) + jnp.log1p(jnp.exp(-jnp.abs(shifted)))
    sig_step = 1.0 / (1.0 + jnp.exp(-shifted))
    rate = -jnp.exp(rate_ref[...])
    tri = (iota((T, T), 0) >= iota((T, T), 1)).astype(F32).astype(BF16)
    triu = (iota((T, T), 0) <= iota((T, T), 1)).astype(F32).astype(BF16)
    lc = sum(dot(tri, part) for part in split3(dt * rate))
    rcol = jnp.log(dt) - lc
    lc_end = lc[T - 1 : T, :]
    r8 = jnp.broadcast_to(reset_ref[...].astype(F32), (8, T)).astype(BF16)
    seg_row = dot(r8, triu)[0:1, :]
    seg_col = dot_t(tri, r8)[:, 0:1]
    seg_end = seg_row[:, T - 1 : T]
    opened = (seg_col == 0.0).astype(F32)
    same_end = (seg_col == seg_end).astype(F32)
    through = jnp.exp(lc_end) * (seg_end == 0.0).astype(F32)
    e_col = jnp.exp(lc) * opened
    taudt = jnp.exp(lc_end - lc) * same_end * dt

    eh = (iota((H, HP), 1) // HEAD_DIM == iota((H, HP), 0)).astype(F32).astype(BF16)
    wide = (iota((H, H * 128), 1) // 128 == iota((H, H * 128), 0)).astype(F32).astype(BF16)
    eye = (iota((H, H), 0) == iota((H, H), 1)).astype(F32).astype(BF16)
    through8 = jnp.broadcast_to(through, (8, H))
    thx = sum(dot(part, eh) for part in split(through8))
    tdx[...] = sum(dot(part, eh) for part in split(taudt))
    for i in range(blocks):
        loc[0, i, STATE : STATE + 8, :] = thx[:, i * CH : (i + 1) * CH]
        loc[1, i, STATE : STATE + 8, :] = thx[:, i * CH : (i + 1) * CH]

    for g in range(G):
        gs = slice(g * STATE, (g + 1) * STATE)
        btr[g] = b_ref[:, gs].astype(F32).T.astype(BF16)
        ctr[g] = c_ref[:, gs].astype(F32).T.astype(BF16)

    def lanes_of(i):
        return pl.ds(pl.multiple_of(i * CH, CH), CH)

    def group_of(i):
        return pl.ds(pl.multiple_of((i // bpg) * STATE, STATE), STATE)

    def heads_of(i):
        first = i * (CH // HEAD_DIM)
        return (iota((H, CH), 1) // HEAD_DIM + first == iota((H, CH), 0)).astype(F32).astype(BF16)

    def local_state(i):
        lanes = lanes_of(i)
        hi, lo = split(tdx[:, lanes] * x_ref[:, lanes].astype(F32))
        xsh_ref[:, lanes] = hi
        xsl_ref[:, lanes] = lo
        bt = btr[i // bpg]
        loc[0, i, 0:STATE, :] = dot(bt, hi) + dot(bt, lo)

    pl.semaphore_wait(barrier, bits + n_head - 1)

    def copy_to(way, slot, k, src, dst, device):
        return pltpu.make_async_remote_copy(
            src_ref=src, dst_ref=dst,
            send_sem=send_sem.at[way, slot, k], recv_sem=recv_sem.at[way, slot, k],
            device_id=device, device_id_type=MESH,
        )

    mate, _ = partner(0)

    def core_copy(way, k):
        return copy_to(way, 0, k, loc.at[way, other * NCH + k], cbuf.at[way, k], {"ctx": mate})

    def step_copy(way, j, k):
        return copy_to(way, j, k, tot.at[way, j - 1, k], rbuf.at[way, j - 1, k], {"ctx": partner(j)[0]})

    def out_copy(way, k):
        return copy_to(way, bits, k, obuf.at[way, k], entry.at[way, core * NCH + k], {"ctx": mate})

    S = STATE

    def exchange(way, produce, work, done):
        own_first = (core == 0) if way == 0 else (core == 1)
        for k in range(NCH):
            produce(other * NCH + k)
            core_copy(way, k).start()
        for k in range(NCH):
            produce(core * NCH + k)
            core_copy(way, k).wait_recv()
            mine = loc[way, core * NCH + k]
            got = cbuf[way, k]
            early = jnp.where(own_first, mine, got)
            late = jnp.where(own_first, got, mine)
            dl = late[S : S + 1, :]
            tot[way, 0, k, 0:S, :] = dl * early[0:S, :] + late[0:S, :]
            tot[way, 0, k, S : S + 8, :] = late[S : S + 8, :] * early[S : S + 8, :]
            step_copy(way, 1, k).start()
        work(0)
        for j in range(1, bits):
            bit = partner(j)[1]
            after = (bit == 1) if way == 0 else (bit == 0)
            for k in range(NCH):
                step_copy(way, j, k).wait_recv()
                got = rbuf[way, j - 1, k]
                if j == 1:
                    base = jnp.where(iota((S + 8, CH), 0) < S, 0.0, 1.0)
                else:
                    base = entry[way, core * NCH + k]
                moved = base[S : S + 1, :] * got
                new = jnp.where(iota((S + 8, CH), 0) < S, moved + base, moved)
                entry[way, core * NCH + k] = jnp.where(after, new, base)
                if j < bits - 1:
                    mine = tot[way, j - 1, k]
                    early = jnp.where(after, got, mine)
                    late = jnp.where(after, mine, got)
                    dl = late[S : S + 1, :]
                    tot[way, j, k, 0:S, :] = dl * early[0:S, :] + late[0:S, :]
                    tot[way, j, k, S : S + 8, :] = late[S : S + 8, :] * early[S : S + 8, :]
                    step_copy(way, j + 1, k).start()
                    if j == 1:
                        work(k + 1)
                else:
                    mine = loc[way, core * NCH + k]
                    theirs = cbuf[way, k]
                    early = jnp.where(own_first, mine, theirs)
                    lead = entry[way, core * NCH + k]
                    trail = early[S : S + 1, :] * lead + early
                    obuf[way, k] = jnp.where(own_first, trail, lead)
                    entry[way, core * NCH + k] = jnp.where(own_first, lead, trail)
                    out_copy(way, k).start()
                    done(core * NCH + k)
            if j == 1:
                work(NCH + 1)
        for k in range(NCH):
            out_copy(way, k).wait_recv()
            done(other * NCH + k)
        for k in range(NCH):
            core_copy(way, k).wait_send()
            for j in range(1, bits):
                step_copy(way, j, k).wait_send()
            out_copy(way, k).wait_send()

    lane = iota((T, 128), 1)
    mask_a = (lane < HEAD_DIM).astype(F32).astype(BF16)
    mask_b = (lane >= HEAD_DIM).astype(F32).astype(BF16)
    pairs = H // 2

    def prepare():
        eexp[...] = sum(dot(part, eh) for part in split(e_col))
        lcrep[...] = sum(dot(part, wide) for part in split3(lc))
        rrep[...] = sum(dot(part, wide) for part in split3(rcol))
        lct[...] = sum(dot_t(eye, part) for part in split3(lc))
        rt[...] = sum(dot_t(eye, part) for part in split3(rcol))
        ok = (iota((T, T), 0) >= iota((T, T), 1)) & (seg_col == seg_row)
        negm[...] = jnp.where(ok, 0.0, -1e30)
        okt = (iota((T, T), 0) <= iota((T, T), 1)) & (seg_col == seg_row)
        negmt[...] = jnp.where(okt, 0.0, -1e30)
        for g in range(G):
            gs = slice(g * STATE, (g + 1) * STATE)
            smat[g] = dot_t(c_ref[:, gs], b_ref[:, gs])
            smatt[g] = dot_t(b_ref[:, gs], c_ref[:, gs])
            dst[g] = jnp.zeros((T, T), F32)

    def column(ref, h):
        col = ref[:, pl.ds(pl.multiple_of(h * 128, 128), 128)]
        return jnp.concatenate([col] * (T // 128), axis=1)

    def forward_pair(j, carry):
        lanes = pl.ds(pl.multiple_of(j * 128, 128), 128)
        xp = x_ref[:, lanes]
        s = smat[(2 * j) // per]
        neg = negm[...]
        y = None
        for half, mask in ((0, mask_a), (1, mask_b)):
            h = 2 * j + half
            w = jnp.exp(column(lcrep, h) + rt[pl.ds(h, 1), :] + neg) * s
            hi, lo = split(w)
            xm = xp * mask
            part = dot(hi, xm) + dot(lo, xm)
            y = part if y is None else y + part
        ybuf[:, lanes] = y
        return carry

    def backward_pair(j, carry):
        lanes = pl.ds(pl.multiple_of(j * 128, 128), 128)
        xp = x_ref[:, lanes]
        dyh = dyh_ref[:, lanes]
        dyl = dyl_ref[:, lanes]
        g = (2 * j) // per
        s = smatt[g]
        neg = negmt[...]
        dx = None
        acc = dst[g]
        for half, mask in ((0, mask_a), (1, mask_b)):
            h = 2 * j + half
            e = jnp.exp(column(rrep, h) + lct[pl.ds(h, 1), :] + neg)
            hi, lo = split(e * s)
            dh = dyh * mask
            part = dot(hi, dh) + dot(hi, dyl * mask) + dot(lo, dh)
            dx = part if dx is None else dx + part
            xm = xp * mask
            acc = acc + (dot_t(xm, dyh) + dot_t(xm, dyl)) * e
        dst[g] = acc
        dxbuf[:, lanes] = dx
        return carry

    def slices(run):
        bounds = [pairs * k // NCH for k in range(NCH + 1)]

        def work(k):
            if 0 < k <= NCH:
                lax.fori_loop(bounds[k - 1], bounds[k], run, 0)

        return work

    forward_work = slices(forward_pair)

    def first_work(k):
        if k == 0:
            prepare()
        forward_work(k)
        if 0 < k <= NCH:
            for i in (2 * k - 2, 2 * k - 1):
                lanes = lanes_of(i)
                gate = gate_ref[:, lanes].astype(F32)
                actb[:, lanes] = gate / (1.0 + jnp.exp(-gate))
                wb[:, lanes] = nw_ref[:, lanes] * go_ref[:, lanes].astype(F32)

    qacc[...] = jnp.zeros((T, CH), F32)
    pacc[...] = jnp.zeros((T, CH), F32)

    def gate_block(i):
        lanes = lanes_of(i)
        cg = c_ref[:, group_of(i)]
        hi, lo = split(entry[0, i, 0:STATE, :])
        y = ybuf[:, lanes] + (dot(cg, hi) + dot(cg, lo)) * eexp[:, lanes]
        ybuf[:, lanes] = y
        gated = (y + x_ref[:, lanes].astype(F32) * skip_ref[:, lanes]) * actb[:, lanes]
        qacc[...] += gated * gated
        pacc[...] += gated * wb[:, lanes]

    exchange(0, local_state, first_work, gate_block)

    q_sum = qacc[...]
    p_sum = pacc[...]
    ones8 = jnp.ones((8, CH), BF16)
    nsend[0:8, :] = sum(dot_t(ones8, part) for part in split3(q_sum))
    nsend[8:16, :] = sum(dot_t(ones8, part) for part in split3(p_sum))

    def norm_copy(d):
        return pltpu.make_async_remote_copy(
            src_ref=nsend, dst_ref=nrecv.at[d - 1],
            send_sem=nsend_sem.at[d - 1], recv_sem=nrecv_sem.at[d - 1],
            device_id={"head": lax.rem(me_h + d, n_head)}, device_id_type=MESH,
        )

    for d in range(1, n_head):
        norm_copy(d).start()
    sums = nsend[...]
    for d in range(1, n_head):
        norm_copy(d).wait_recv()
        sums = sums + nrecv[d - 1]
    inv_row = lax.rsqrt(sums[0:1, :] / width + EPSILON)
    coef_row = inv_row * inv_row * inv_row * sums[8:9, :] / width
    inv = jnp.broadcast_to(inv_row, (128, T)).T
    coef = jnp.broadcast_to(coef_row, (128, T)).T
    if CH > 128:
        inv = jnp.concatenate([inv] * (CH // 128), axis=1)
        coef = jnp.concatenate([coef] * (CH // 128), axis=1)

    def adjoint_block(i):
        lanes = lanes_of(i)
        act = actb[:, lanes]
        gated = (ybuf[:, lanes] + x_ref[:, lanes].astype(F32) * skip_ref[:, lanes]) * act
        dy = (inv * wb[:, lanes] - gated * coef) * act
        dybuf[:, lanes] = dy
        dyh_ref[:, lanes], dyl_ref[:, lanes] = split(dy)
        hi, lo = split(dy * eexp[:, lanes])
        edh_ref[:, lanes] = hi
        edl_ref[:, lanes] = lo
        ct = ctr[i // bpg]
        loc[1, i, 0:STATE, :] = dot(ct, hi) + dot(ct, lo)

    dyya[...] = jnp.zeros((T, H), F32)
    xdxa[...] = jnp.zeros((T, H), F32)

    def gate_grad(i):
        lanes = lanes_of(i)
        y = ybuf[:, lanes]
        core_out = y + x_ref[:, lanes].astype(F32) * skip_ref[:, lanes]
        gate = gate_ref[:, lanes].astype(F32)
        sig = 1.0 / (1.0 + jnp.exp(-gate))
        ggated = inv * wb[:, lanes] - core_out * actb[:, lanes] * coef
        gg_ref[:, lanes] = (ggated * core_out * sig * (1.0 + gate * (1.0 - sig))).astype(BF16)
        dyya[...] += sum(dot_t(part, heads_of(i)) for part in split(dybuf[:, lanes] * y))

    backward_work = slices(backward_pair)

    def second_work(k):
        backward_work(k)
        if k == 0:
            for i in range(NCH // 2):
                gate_grad(i)
        elif k <= NCH:
            gate_grad(NCH // 2 + k - 1)
        else:
            for i in range(NCH + NCH // 2, 2 * NCH):
                gate_grad(i)
            for g in range(G):
                gs = slice(g * STATE, (g + 1) * STATE)
                acc = dst[g]
                hi, lo = split(acc)
                cg = c_ref[:, gs]
                gb_ref[:, gs] = dot(hi, cg) + dot(lo, cg)
                hi, lo = split(acc.T)
                bg = b_ref[:, gs]
                gc = dot(hi, bg) + dot(lo, bg)
                for i in range(g * bpg, (g + 1) * bpg):
                    lanes = lanes_of(i)
                    hi, lo = split(entry[0, i, 0:STATE, :])
                    edh = edh_ref[:, lanes]
                    gc = gc + dot_t(edh, hi) + dot_t(edh, lo) + dot_t(edl_ref[:, lanes], hi)
                gc_ref[:, gs] = gc

    ends_of = []

    def input_block(i):
        lanes = lanes_of(i)
        gs = group_of(i)
        bg = b_ref[:, gs]
        adj = entry[1, i, 0:STATE, :]
        hi, lo = split(adj)
        xsh = xsh_ref[:, lanes]
        gb_ref[:, gs] += dot_t(xsh, hi) + dot_t(xsh, lo) + dot_t(xsl_ref[:, lanes], hi)
        dx = dxbuf[:, lanes] + (dot(bg, hi) + dot(bg, lo)) * tdx[:, lanes]
        gx_ref[:, lanes] = (dx + dybuf[:, lanes] * skip_ref[:, lanes]).astype(BF16)
        eb = heads_of(i)
        xdxa[...] += sum(dot_t(part, eb) for part in split(dx * x_ref[:, lanes].astype(F32)))
        local = loc[0, i]
        leaving = local[S : S + 1, :] * entry[0, i, 0:STATE, :] + local[0:S, :]
        col = jnp.broadcast_to(jnp.sum(adj * leaving, axis=0, keepdims=True), (8, CH))
        ends_of.append(sum(dot_t(part, eb) for part in split3(col)))

    exchange(1, adjoint_block, second_work, input_block)
    ends = sum(ends_of)
    xdx = xdxa[...]
    dyy = dyya[...]
    rc = sum(dot(triu, part) for part in split3(dyy - xdx)) + ends[0:1, :]
    gs_ref[...] = (xdx / dt + rate * rc) * sig_step

    for d in range(1, n_head):
        norm_copy(d).wait_send()


def body(mesh_shape, x, gate, step, b, c, bias, rate, skip, nw, resets, go):
    n_ctx, n_head = mesh_shape
    T, HP = x.shape
    H = step.shape[1]
    G = b.shape[1] // STATE
    bits = n_ctx.bit_length() - 1
    CH = HP // (2 * NCH)
    R = STATE + 8
    vm = pltpu.VMEM
    skip_cols = jnp.repeat(skip, HEAD_DIM)[None, :]
    return pl.pallas_call(
        functools.partial(kernel, n_ctx, n_head, HP * n_head),
        out_shape=(
            jax.ShapeDtypeStruct((T, HP), BF16),
            jax.ShapeDtypeStruct((T, HP), BF16),
            jax.ShapeDtypeStruct((T, H), F32),
            jax.ShapeDtypeStruct((T, G * STATE), F32),
            jax.ShapeDtypeStruct((T, G * STATE), F32),
        ),
        in_specs=[pl.BlockSpec(memory_space=pltpu.VMEM)] * 11,
        out_specs=[pl.BlockSpec(memory_space=pltpu.VMEM)] * 5,
        scratch_shapes=[
            vm((2, 2 * NCH, R, CH), F32),
            vm((2, NCH, R, CH), F32),
            vm((2, bits - 1, NCH, R, CH), F32),
            vm((2, bits - 1, NCH, R, CH), F32),
            vm((2, NCH, R, CH), F32),
            vm((2, 2 * NCH, R, CH), F32),
            vm((T, H * 128), F32),
            vm((T, H * 128), F32),
            vm((H, T), F32),
            vm((H, T), F32),
            vm((T, T), F32),
            vm((T, T), F32),
            vm((G, T, T), F32),
            vm((G, T, T), F32),
            vm((G, T, T), F32),
            vm((T, HP), F32),
            vm((T, HP), F32),
            vm((T, HP), BF16),
            vm((T, HP), BF16),
            vm((T, HP), BF16),
            vm((T, HP), BF16),
            vm((T, HP), BF16),
            vm((T, HP), BF16),
            vm((T, HP), F32),
            vm((T, HP), F32),
            vm((T, HP), F32),
            vm((G, STATE, T), BF16),
            vm((G, STATE, T), BF16),
            vm((T, HP), F32),
            vm((T, HP), F32),
            vm((T, CH), F32),
            vm((T, CH), F32),
            vm((T, H), F32),
            vm((T, H), F32),
            vm((16, T), F32),
            vm((max(n_head - 1, 1), 16, T), F32),
            pltpu.SemaphoreType.DMA((2, bits + 1, NCH)),
            pltpu.SemaphoreType.DMA((2, bits + 1, NCH)),
            pltpu.SemaphoreType.DMA((max(n_head - 1, 1),)),
            pltpu.SemaphoreType.DMA((max(n_head - 1, 1),)),
        ],
        compiler_params=pltpu.CompilerParams(
            collective_id=0, has_side_effects=True, vmem_limit_bytes=60 * 1024 * 1024
        ),
    )(
        x, gate, step, b, c, bias[None, :], rate[None, :], skip_cols, nw[None, :], resets[None, :], go
    )


def solution(mesh):
    return jax.shard_map(
        functools.partial(body, (mesh.shape["ctx"], mesh.shape["head"])),
        mesh=mesh,
        in_specs=(
            P("ctx", "head"), P("ctx", "head"), P("ctx", "head"), P("ctx", "head"), P("ctx", "head"),
            P("head"), P("head"), P("head"), P("head"), P("ctx"), P("ctx", "head"),
        ),
        out_specs=(P("ctx", "head"),) * 5,
        check_vma=False,
    )
```
